1024 devices in a mesh: dp: 8 (over x, z_hi), ctx: 16 (over y, core), tp: 8 (over z_lo).
Axes of the slice: x: 4, y: 8, z: 16 (z_hi: 2, z_lo: 8; z = z_hi * 8 + z_lo), core: 2. Of those that a mesh axis runs over, the one named last changes fastest.
Arguments:
- tokens: bfloat16 [16384, 2048], P(('dp', 'ctx'), 'tp'), may hold values from -6 to 6
- grad_out: bfloat16 [16384, 2048], P(('dp', 'ctx'), 'tp'), may hold values from -1.5 to 1.5
- expert_ids: int32 [16384, 8], P(('dp', 'ctx')), may hold values from 0 to 127, all different within a row; in each aligned block of 128 rows (0 to 127, 128 to 255, ...) at most 10 rows name the same one
- gate_weights: float32 [16384, 8], P(('dp', 'ctx')), may hold values from 0.03 to 0.5
- gate_proj: bfloat16 [128, 2048, 768], P(('ctx', 'tp')), may hold values from -0.125 to 0.125
- up_proj: bfloat16 [128, 2048, 768], P(('ctx', 'tp')), may hold values from -0.125 to 0.125
- down_proj: bfloat16 [128, 768, 2048], P(('ctx', 'tp')), may hold values from -0.21875 to 0.21875
Outputs:
- combined: bfloat16 [16384, 2048], P(('dp', 'ctx'), 'tp')
- grad_tokens: bfloat16 [16384, 2048], P(('dp', 'ctx'), 'tp')
- grad_gate: float32 [16384, 8], P(('dp', 'ctx'))
- grad_down: bfloat16 [128, 768, 2048], P(('ctx', 'tp'), 'dp')
The draws below stay inside these ranges and needn't reach their ends.
Inputs may be any that keep to these rules, and one draw needn't show every extreme that they name: `expert_ids`: each row names 8 different experts. Among the 128 rows of one token group no expert is named more than 10 times, and in every draw some group names some expert exactly 10 times.
All inputs are finite; a program needn't handle non-finite values.
Results may differ from the reference program's by a relative error of at most 0.017.
Values may be sent and summed in bfloat16 or wider, within the bound.
No kernel may reach another device: no remote copies, remote signals or barrier semaphores. Data moves between devices by JAX's collectives and lax.ppermute only.
A program may use at most 64 MiB of HBM per device.

```python
import math
import jax
import jax.numpy as jnp
import numpy as np
from jax import lax

D = 2048
FF = 768
TOPK = 8
TOK = 128
EXPERTS = 128
CAP = 10
TOKENS = 16384
N_DP = 8
N_CTX = 16


def block_scale(key, dims, shards, smallest, largest):
    loudness, own = 1.0, jax.random.fold_in(key, 6)
    for dim, shards_of in shards:
        steps = jnp.exp(jax.random.uniform(jax.random.fold_in(own, dim), (shards_of,), jnp.float32, smallest / len(shards), largest / len(shards)))
        loudness = loudness * jnp.repeat(steps, dims[dim] // shards_of).reshape([-1 if axis == dim else 1 for axis in range(len(dims))])
    return loudness


def assign_block(stream_key, own, number, rows, count, top, bound, skew):
    ranking = jax.random.permutation(stream_key, count)
    crowded, ordinary = portions_of(count, rows * top, bound, skew, True), portions_of(count, rows * top, bound, skew, False)
    places = jnp.arange(count)

    def named(lengths, offset_by):
        used = int((lengths > 0).sum())
        fixed = max(1, used // 4)
        moved = fixed + (places - fixed + offset_by * (used - fixed)) % max(1, count - fixed)
        return jnp.zeros((count,), jnp.int32).at[ranking[jnp.where(places < fixed, places, moved)]].set(jnp.asarray(lengths, jnp.int32))

    lengths = jnp.where(number % 4 == 0, named(crowded, number // 4), named(ordinary, number - number // 4 - 1))
    mixed = jax.random.permutation(jax.random.fold_in(own, 3), count)
    giver, receiver = mixed[0:count // 2 * 2:2], mixed[1:count // 2 * 2:2]
    margin = jnp.minimum(lengths[giver] - 1, bound - lengths[receiver]) // 2
    margin = jnp.where((giver == ranking[0]) | (receiver == ranking[0]) | (lengths[receiver] == 0), 0, jnp.maximum(margin, 0))
    moved = jax.random.randint(jax.random.fold_in(own, 4), (count // 2,), 0, 1 << 20) % (margin + 1)
    lengths = lengths.at[giver].add(-moved).at[receiver].add(moved)
    labels = jnp.searchsorted(jnp.cumsum(lengths), jnp.arange(rows * top), side="right").astype(jnp.int32)
    grid = labels.reshape(top, rows).T
    grid = grid[jax.random.permutation(jax.random.fold_in(own, 1), rows)]
    offset_by = jax.random.randint(jax.random.fold_in(own, 2), (rows, 1), 0, top)
    return jnp.take_along_axis(grid, (jnp.arange(top)[None, :] + offset_by) % top, axis=1)


def portions_of(amount, total, reach, skew, full):
    loads = [(1 << 20) // math.isqrt(rank ** skew) + 1 for rank in range(1, amount + 1)]
    largest = reach if full else min(reach, max(-(-total // amount), total * loads[0] // sum(loads)))
    least = 1 if total - largest >= amount - 1 else 0
    counts, surplus = [largest] + [least] * (amount - 1), total - largest - least * (amount - 1)
    while surplus > 0:
        movable = [i for i in range(1, amount) if counts[i] < largest] or [i for i in range(1, amount) if counts[i] < reach]
        whole, remaining = sum([loads[i] for i in movable]), surplus
        for i in movable:
            extra = min(reach - counts[i], max(1, remaining * loads[i] // whole), surplus)
            counts[i] = counts[i] + extra
            surplus = surplus - extra
    return np.array(counts)


def normal_values(rng, dims, spread, bound, cuts=(), kind=jnp.bfloat16):
    array = spread * jax.random.normal(rng, dims, jnp.float32)
    if cuts:
        array = array * block_scale(rng, dims, cuts, -0.22, 0.18)
    return jnp.clip(array, -bound, bound).astype(kind)


def setup_inputs(seed: int = 0) -> dict:
    keys = jax.random.split(jax.random.key(seed), 8)
    tokens = normal_values(keys[0], (TOKENS, D), 1.0, 6.0, ((0, 128), (1, 8)))
    grad_out = normal_values(keys[1], (TOKENS, D), 0.25, 1.5, ((0, 128), (1, 8)))
    expert_ids_keys = jax.random.split(jax.random.fold_in(keys[2], 1), TOKENS // TOK)
    expert_ids_turns = jax.random.permutation(jax.random.fold_in(keys[2], 3), TOKENS // TOK)
    expert_ids = jax.vmap(lambda own, number: assign_block(jax.random.fold_in(keys[2], 2), own, number, TOK, EXPERTS, TOPK, CAP, 1))(expert_ids_keys, expert_ids_turns).reshape((TOKENS, TOPK))
    gate_weights = jnp.clip(jnp.exp(math.log(0.5) - 2.8134107 * jax.random.uniform(keys[3], (TOKENS, TOPK), jnp.float32) ** block_scale(keys[3], (TOKENS, TOPK), ((0, 128),), -0.2, 0.2)), 0.03, 0.5)
    gate_proj = normal_values(keys[4], (EXPERTS, D, FF), D ** -0.5, 0.125, ((0, 128),))
    up_proj = normal_values(keys[5], (EXPERTS, D, FF), D ** -0.5, 0.125, ((0, 128),))
    down_proj = normal_values(keys[6], (EXPERTS, FF, D), FF ** -0.5, 0.21875, ((0, 128),))
    return {"tokens": tokens, "grad_out": grad_out, "expert_ids": expert_ids, "gate_weights": gate_weights, "gate_proj": gate_proj, "up_proj": up_proj, "down_proj": down_proj}


def pick_slots(choices):
    expert_range = jnp.arange(EXPERTS, dtype=jnp.int32)
    onehot = (choices[..., None] == expert_range).astype(jnp.int32)
    earlier = jnp.cumsum(onehot, axis=-2) - onehot
    return jnp.sum(earlier * onehot, axis=-1).astype(jnp.int32)


def reference(tokens, grad_out, expert_ids, gate_weights, gate_proj, up_proj, down_proj):
    groups = N_DP * N_CTX
    choices = expert_ids.reshape(groups, TOK * TOPK).astype(jnp.int32)
    gain_rows = gate_weights.reshape(groups, TOK * TOPK)
    slot_index = pick_slots(choices)
    group_index = jnp.broadcast_to(jnp.arange(groups, dtype=jnp.int32)[:, None], choices.shape)
    token_index = group_index * TOK + (jnp.arange(TOK * TOPK, dtype=jnp.int32) // TOPK)[None, :]
    holder = jnp.full((EXPERTS, groups, CAP), groups * TOK, dtype=jnp.int32)
    holder = holder.at[choices, group_index, slot_index].set(token_index)
    slot_gain = jnp.zeros((EXPERTS, groups, CAP), dtype=gate_weights.dtype)
    slot_gain = slot_gain.at[choices, group_index, slot_index].set(gain_rows)
    padded_x = jnp.concatenate([tokens, jnp.zeros((1, D), dtype=tokens.dtype)], axis=0)
    padded_dy = jnp.concatenate([grad_out, jnp.zeros((1, D), dtype=grad_out.dtype)], axis=0)

    def expert_step(operands):
        row_index, gain_slots, gate_weight, up_weight, down_weight = operands
        flat_index = row_index.reshape(-1)
        expert_rows = jnp.take(padded_x, flat_index, axis=0)
        dy_rows = jnp.take(padded_dy, flat_index, axis=0).astype(jnp.float32)
        scaled_dy = (gain_slots.reshape(-1)[:, None] * dy_rows).astype(jnp.bfloat16)
        gate_act = jnp.dot(expert_rows, gate_weight, preferred_element_type=jnp.float32)
        up_act = jnp.dot(expert_rows, up_weight, preferred_element_type=jnp.float32)
        sigmoid_gate = jax.nn.sigmoid(gate_act)
        hidden = (gate_act * sigmoid_gate * up_act).astype(jnp.bfloat16)
        expert_out = jnp.dot(hidden, down_weight, preferred_element_type=jnp.float32).astype(jnp.bfloat16)
        d_hidden = jnp.dot(scaled_dy, down_weight.T, preferred_element_type=jnp.float32)
        d_gate = (d_hidden * up_act * sigmoid_gate * (1.0 + gate_act * (1.0 - sigmoid_gate))).astype(jnp.bfloat16)
        d_up = (d_hidden * gate_act * sigmoid_gate).astype(jnp.bfloat16)
        dx_rows = (jnp.dot(d_gate, gate_weight.T, preferred_element_type=jnp.float32)
                   + jnp.dot(d_up, up_weight.T, preferred_element_type=jnp.float32)).astype(jnp.bfloat16)
        hidden_parts = hidden.reshape(N_DP, N_CTX * CAP, FF).astype(jnp.float32)
        dy_parts = scaled_dy.reshape(N_DP, N_CTX * CAP, D).astype(jnp.float32)
        partial_value = jnp.einsum("rnf,rnd->rfd", hidden_parts, dy_parts).astype(jnp.bfloat16)
        grad_down = jnp.sum(partial_value.astype(jnp.float32), axis=0).astype(jnp.bfloat16)
        return expert_out, dx_rows, grad_down

    expert_out, dx_rows, grad_down = lax.map(expert_step, (holder, slot_gain, gate_proj, up_proj, down_proj))
    out_flat = expert_out.reshape(EXPERTS * groups * CAP, D)
    dx_flat = dx_rows.reshape(EXPERTS * groups * CAP, D)
    positions = ((choices * groups + group_index) * CAP + slot_index).astype(jnp.int32)

    def combine_group(operands):
        position_row, gain_row, dy_block = operands
        picked_out = jnp.take(out_flat, position_row, axis=0).reshape(TOK, TOPK, D).astype(jnp.float32)
        picked_dx = jnp.take(dx_flat, position_row, axis=0).reshape(TOK, TOPK, D).astype(jnp.float32)
        combined = jnp.sum(gain_row.reshape(TOK, TOPK)[:, :, None] * picked_out, axis=1).astype(jnp.bfloat16)
        grad_gate = jnp.sum(dy_block.astype(jnp.float32)[:, None, :] * picked_out, axis=2)
        grad_tokens = jnp.sum(picked_dx, axis=1).astype(jnp.bfloat16)
        return combined, grad_tokens, grad_gate

    combined, grad_tokens, grad_gate = lax.map(combine_group, (positions, gain_rows, grad_out.reshape(groups, TOK, D)))
    return (combined.reshape(groups * TOK, D), grad_tokens.reshape(groups * TOK, D),
            grad_gate.reshape(groups * TOK, TOPK), grad_down)
```

```python
import functools

import jax
import jax.numpy as jnp
from jax import lax
from jax.experimental import pallas as pl
from jax.experimental.pallas import tpu as pltpu
from jax.sharding import PartitionSpec as P

BF = jnp.bfloat16
F32 = jnp.float32
MAIN = 8
REST = 2
QUAD = 4
VMEM = 60 * 1024 * 1024


def iota(shape, dim):
    return lax.broadcasted_iota(jnp.int32, shape, dim)


def dot(a, b):
    return jnp.dot(a, b, preferred_element_type=F32)


def dot_nt(a, b):
    return lax.dot_general(a, b, (((1,), (1,)), ((), ())), preferred_element_type=F32)


def routing(ids_t, gates_t, lane):
    top, tokens = ids_t.shape
    rows = (MAIN + REST) * 16
    row = iota((rows, tokens), 0)
    left = row - MAIN * 16
    expert = jnp.where(left < 0, row >> 3, left >> 1) * 8 + lane
    slot = jnp.where(left < 0, row & 7, MAIN + (left & 1)).astype(F32)
    named = jnp.zeros((rows, tokens), F32)
    weight = jnp.zeros((rows, tokens), F32)
    for k in range(top):
        hit = ids_t[k : k + 1, :] == expert
        named = named + jnp.where(hit, 1.0, 0.0)
        weight = weight + jnp.where(hit, gates_t[k : k + 1, :], 0.0)
    before = jnp.where(iota((tokens, tokens), 0) < iota((tokens, tokens), 1), 1.0, 0.0)
    earlier = dot(named.astype(BF), before.astype(BF))
    holds = (named > 0.5) & (earlier == slot)
    return holds, weight, expert


def rest_mix():
    p, q = iota((256, 256), 0), iota((256, 256), 1)
    return jnp.where(q == ((p >> 1) & 7) * 32 + (p >> 4) * 2 + (p & 1), 1.0, 0.0).astype(BF)


def rest_unmix():
    q, p = iota((256, 256), 0), iota((256, 256), 1)
    return jnp.where(p == ((q >> 1) & 15) * 16 + (q >> 5) * 2 + (q & 1), 1.0, 0.0).astype(BF)


def fold(send_ref, shard, first, second):
    split = MAIN * 16
    tiles = [v[:split].reshape(16, MAIN, 256) for v in (first, second)]
    send_ref[:, shard * 16 : (shard + 1) * 16, :] = jnp.concatenate(tiles, axis=1).astype(BF)
    return [first[split:].astype(BF), second[split:].astype(BF)]


def fold_rest(send_ref, rest):
    mixed = dot(rest_mix(), jnp.concatenate(rest, axis=0))
    send_ref[:, QUAD * 16 : QUAD * 20, :] = mixed.reshape(16, 16, 256).astype(BF)


def unfold(recv_ref):
    tail = recv_ref[:, QUAD * 16 : QUAD * 20, :].astype(F32).reshape(256, 256).astype(BF)
    rest = dot(rest_unmix(), tail)
    out = []
    for shard in range(QUAD):
        both = recv_ref[:, shard * 16 : (shard + 1) * 16, :].astype(F32)
        pair = []
        for a in range(2):
            tiles = both[:, a * MAIN : (a + 1) * MAIN, :].reshape(MAIN * 16, 256)
            at = (shard * 2 + a) * 32
            pair.append(jnp.concatenate([tiles, rest[at : at + 32]], axis=0).astype(BF))
        out.append(pair)
    return out


def dispatch_kernel(where_ref, ids_ref, gates_ref, p0, p1, p2, p3, send_ref):
    holds, weight, _ = routing(ids_ref[...], gates_ref[...], where_ref[0])
    pick = jnp.where(holds, 1.0, 0.0).astype(BF)
    gain = jnp.sum(jnp.where(holds, weight, 0.0), axis=1, keepdims=True)
    rest = []
    for shard, ref in enumerate((p0, p1, p2, p3)):
        x_rows = dot(pick, ref[:128, :])
        dy_rows = dot(pick, ref[128:, :]) * gain
        rest += fold(send_ref, shard, x_rows, dy_rows)
    fold_rest(send_ref, rest)


def shard_at(where_ref, far, shard):
    return pl.multiple_of(((where_ref[0] ^ (far * QUAD)) ^ shard) * 256, 256)


def fetch(where_ref, far, weights, held, sems, first=0):
    copies = []
    for shard in range(QUAD):
        at = pl.ds(shard_at(where_ref, far, shard), 256)
        parts = [w.at[at, :] for w in weights[:2]] + [w.at[:, at] for w in weights[2:]]
        trio = [
            pltpu.make_async_copy(src, dst.at[shard], sems.at[shard, first + n])
            for n, (src, dst) in enumerate(zip(parts, held))
        ]
        for copy in trio:
            copy.start()
        copies.append(trio)
    return copies


def inward(recv_ref, copies, held, dy_list, sums):
    gate, up, d_hidden = sums
    wg, wu, wd = held[:3]
    for shard, (x_rows, dy_rows) in enumerate(unfold(recv_ref)):
        dy_list.append(dy_rows)
        for copy in copies[shard]:
            copy.wait()
        gate = gate + dot(x_rows, wg[shard])
        up = up + dot(x_rows, wu[shard])
        d_hidden = d_hidden + dot_nt(dy_rows, wd[shard])
    return gate, up, d_hidden


def outward(outs, d_gate, d_up, copies, held, send_ref):
    wg, wu = held[:2]
    rest = []
    for shard in range(QUAD):
        if copies is not None:
            for copy in copies[shard]:
                copy.wait()
        dx = dot_nt(d_gate, wg[shard]) + dot_nt(d_up, wu[shard])
        rest += fold(send_ref, shard, outs[shard], dx)
    fold_rest(send_ref, rest)


def tail_pick(turn):
    p, q = (0, 1) if turn else (1, 0)
    shape = (128, 32) if turn else (32, 128)
    row, rest = iota(shape, p), iota(shape, q)
    return jnp.where(((row >> 3) == (rest >> 1)) & ((row & 7) == (rest & 1)), 1.0, 0.0).astype(BF)


def near_kernel(where_ref, recv_ref, *refs):
    weights, held, sems = refs[:3], refs[7:10], refs[10]
    gate_ref, up_ref, dh_ref, dy_ref = refs[3:7]
    copies = fetch(where_ref, 0, weights, held, sems)
    zero = jnp.zeros(gate_ref.shape, F32)
    dy_rows = []
    gate_ref[...], up_ref[...], dh_ref[...] = inward(
        recv_ref, copies, held, dy_rows, (zero, zero, zero)
    )
    for shard, rows in enumerate(dy_rows):
        dy_ref[shard] = rows


def far_kernel(where_ref, recv_ref, gate_ref, up_ref, dh_ref, near_ref, *refs):
    weights, outs, held, sems, block = refs[:3], refs[3:12], refs[12:16], refs[16], refs[17]
    home_ref, dgate_ref, dup_ref, send_ref, partial_ref = outs[:5]
    copies = fetch(where_ref, 1, weights, held[:3], sems)
    wd_near = []
    for shard in range(QUAD):
        at = pl.ds(shard_at(where_ref, 0, shard), 256)
        copy = pltpu.make_async_copy(weights[2].at[:, at], held[3].at[shard], sems.at[shard, 3])
        copy.start()
        wd_near.append(copy)
    dy_rows = []
    gate, up, d_hidden = inward(
        recv_ref, copies, held, dy_rows, (gate_ref[...], up_ref[...], dh_ref[...])
    )
    s = jax.nn.sigmoid(gate)
    hidden32 = gate * s * up
    hidden = hidden32.astype(BF)
    d_gate = (d_hidden * up * s * (1.0 + gate * (1.0 - s))).astype(BF)
    d_up = (d_hidden * gate * s).astype(BF)
    dgate_ref[...] = d_gate
    dup_ref[...] = d_up
    far_outs = [dot(hidden, held[2][shard]) for shard in range(QUAD)]
    outward(far_outs, d_gate, d_up, None, held, send_ref)
    dots = jnp.zeros((gate.shape[0], 1), F32)
    for shard in range(QUAD):
        wd_near[shard].wait()
        out = dot(hidden, held[3][shard]).astype(BF)
        home_ref[shard] = out
        for rows, dy in ((out, near_ref[shard]), (far_outs[shard].astype(BF), dy_rows[shard])):
            dots = dots + jnp.sum(rows.astype(F32) * dy.astype(F32), axis=1, keepdims=True)
    high = dots.astype(BF).astype(F32)
    terms = jnp.where(iota((dots.shape[0], 256), 1) < 128, high, dots - high)
    tail = dot(tail_pick(True), terms[MAIN * 16 :].astype(BF))
    terms = [v.reshape(16, 8, 256) for v in (terms[: MAIN * 16], tail)]
    send_ref[:, QUAD * 20 :, :] = jnp.concatenate(terms, axis=1).astype(BF)
    turned = hidden32.T.astype(BF)
    for shard in range(QUAD):
        at = slice(shard * 256, (shard + 1) * 256)
        partial_ref[:, at] = dot(turned, dy_rows[shard]).astype(BF)
        block[:, at] = dot(turned, near_ref[shard]).astype(BF)
    for n, ref in enumerate(outs[5:]):
        ref[...] = block[pl.ds(pl.multiple_of((where_ref[2] ^ n) * 192, 192), 192), :]


def back_kernel(where_ref, home_ref, dgate_ref, dup_ref, *refs):
    weights, send_ref, held, sems = refs[:2], refs[2], refs[3:5], refs[5]
    copies = fetch(where_ref, 0, weights, held, sems)
    outs = [home_ref[shard].astype(F32) for shard in range(QUAD)]
    outward(outs, dgate_ref[...], dup_ref[...], copies, held, send_ref)


def split_lines(lines):
    high = lines.astype(BF).astype(F32)
    middle = (lines - high).astype(BF).astype(F32)
    low = lines - high - middle
    pairs = [jnp.concatenate(v, axis=1) for v in ((high, middle), (low, jnp.zeros_like(low)))]
    return jnp.concatenate(pairs, axis=0).astype(BF)


def join_lines(ref):
    terms = ref[256:, :].astype(F32)
    return terms[:8, :128] + terms[:8, 128:] + terms[8:, :128]


def first_kernel(where_ref, ids_ref, gates_ref, recv_ref, next_ref, *outs):
    outs[-1][...] = next_ref[...]
    combine_kernel(True, where_ref, ids_ref, gates_ref, recv_ref, *outs[:-1])


def combine_kernel(first, where_ref, ids_ref, gates_ref, recv_ref, *outs):
    holds, weight, expert = routing(ids_ref[...], gates_ref[...], where_ref[0])
    gains = jnp.where(holds, weight, 0.0)
    picks = jnp.where(holds, 1.0, 0.0).T.astype(BF)
    turned = gains.T
    high = turned.astype(BF)
    low = (turned - high.astype(F32)).astype(BF)
    for (out, dx), to in zip(unfold(recv_ref), outs):
        to[:128, :] = (dot(high, out) + dot(low, out)).astype(BF)
        to[128:256, :] = dot(picks, dx).astype(BF)
    if not first:
        return
    terms = recv_ref[:, QUAD * 20 :, :].astype(F32)
    main, tail = [terms[:, n * 8 : (n + 1) * 8, :].reshape(128, 256) for n in range(2)]
    terms = jnp.concatenate([main, dot(tail_pick(False), tail.astype(BF))], axis=0)
    dots = terms[:, :1] + terms[:, 128:129]
    gain = jnp.sum(gains, axis=1, keepdims=True)
    slopes = jnp.where(gain > 0.0, dots / jnp.where(gain > 0.0, gain, 1.0), 0.0)
    sums = jnp.where(holds, slopes, 0.0)
    ids = ids_ref[...]
    lines = [
        jnp.sum(jnp.where(ids[k : k + 1, :] == expert, sums, 0.0), axis=0, keepdims=True)
        for k in range(ids.shape[0])
    ]
    lines = split_lines(jnp.concatenate(lines, axis=0))
    for to in outs:
        to[256:, :] = lines


def end_kernel(where_ref, sum_ref, *refs):
    for flip, to in enumerate(refs[-2:]):
        rows = pl.ds(pl.multiple_of((where_ref[1] ^ flip) * 96, 96), 96)
        total = refs[0][rows, :].astype(F32)
        for ref in refs[1:-2]:
            total = total + ref[rows, :].astype(F32)
        to[:, : QUAD * 256] = total.astype(BF)
        to[:, QUAD * 256 :] = sum_ref[rows, :]


def total_of(refs):
    total = refs[0][:256, :].astype(F32)
    for ref in refs[1:]:
        total = total + ref[:256, :].astype(F32)
    return total.astype(BF)


def total_kernel(where_ref, *refs):
    refs[-1][:256, :] = total_of(refs[:-1])
    lines = join_lines(refs[0])
    for ref in refs[1:-1]:
        lines = lines + join_lines(ref)
    refs[-1][256:, :] = split_lines(lines)


def last_kernel(where_ref, mine_ref, other_ref, *refs):
    total = total_of((other_ref, *refs[:-3]))
    refs[-3][...] = total[:128]
    refs[-2][...] = total[128:]
    refs[-1][...] = join_lines(mine_ref) + join_lines(other_ref)


def add_kernel(where_ref, held_ref, got_ref, out_ref):
    for n in range(2 * QUAD):
        at = slice(n * 256, (n + 1) * 256)
        total = held_ref[:, at].astype(F32) + got_ref[:, at].astype(F32)
        out_ref[:, pl.ds(shard_at(where_ref, n // QUAD, n % QUAD), 256)] = total.astype(BF)


def whole(shape):
    return pl.BlockSpec(shape, lambda i: (0,) * len(shape))


def call(kernel, outs, micros, scalars, *operands, weights=(), downs=0, more=(), after=()):
    specs = [pl.BlockSpec(memory_space=pltpu.SMEM)] + [whole(v.shape) for v in operands]
    specs += [pl.BlockSpec(memory_space=pl.ANY) for _ in (*weights, *after)]
    first = 1 + len(operands) + len(weights)
    last = first + len(after)

    def body(*refs):
        kernel(*refs[:first], *refs[last:])

    scratch = []
    if weights:
        wide = weights[0].shape[1]
        scratch = [pltpu.VMEM((QUAD, 256, wide), BF) for _ in weights[:2]]
        scratch += [pltpu.VMEM((QUAD, wide, 256), BF) for _ in range(downs)]
        scratch += [pltpu.SemaphoreType.DMA((QUAD, len(scratch)))]
    shapes = [jax.ShapeDtypeStruct(s, d) for s, d in outs]
    results = pl.pallas_call(
        body,
        grid=(1,),
        out_shape=shapes,
        in_specs=specs,
        out_specs=[whole(v.shape) for v in shapes],
        scratch_shapes=[*scratch, *more],
        compiler_params=pltpu.CompilerParams(vmem_limit_bytes=VMEM),
        cost_estimate=pl.CostEstimate(
            flops=micros * 10**9, bytes_accessed=micros * 3 * 10**6, transcendentals=0
        ),
    )(scalars, *operands, *weights, *after)
    return results[0] if len(results) == 1 else results


def swap(value, axis, bit):
    size = lax.axis_size(axis)
    return lax.ppermute(value, axis, [(i, i ^ bit) for i in range(size)])


def over_ctx(value):
    return lax.all_to_all(value, "ctx", split_axis=0, concat_axis=0, tiled=True)


def shards(tokens, grad_out, expert_ids, gate_weights, gate_proj, up_proj, down_proj):
    dp, lane = lax.axis_index("dp"), lax.axis_index("tp")
    scalars = jnp.stack([lane, dp & 1, dp >> 1]).astype(jnp.int32)
    wg, wu, wd = gate_proj[0], up_proj[0], down_proj[0]
    width, hidden_width = wg.shape
    ids_t, gates_t = expert_ids.T, gate_weights.T
    table = (scalars, ids_t, gates_t)
    slots = (MAIN + REST) * 16
    travel = (16, QUAD * 20, 256)

    own = jnp.concatenate([tokens, grad_out], axis=0)
    across = swap(own, "tp", 4)
    near = [own] + [swap(own, "tp", d) for d in (1, 2, 3)]
    far = [across] + [swap(across, "tp", d) for d in (1, 2, 3)]

    send_near = call(dispatch_kernel, [(travel, BF)], 4, *table, *near, after=(across,))
    got_near = over_ctx(send_near)
    send_far = call(dispatch_kernel, [(travel, BF)], 4, *table, *far, after=(send_near,))
    got_far = over_ctx(send_far)

    sums = ((slots, hidden_width), F32)
    dy_shape = ((QUAD, slots, 256), BF)
    act = ((slots, hidden_width), BF)
    gate, up, d_hidden, dy_near = call(
        near_kernel, [sums, sums, sums, dy_shape], 5, scalars, got_near,
        weights=(wg, wu, wd), downs=1, after=(send_far,),
    )
    longer = (16, QUAD * 20 + 16, 256)
    home, d_gate, d_up, back_far, partial, *blocks = call(
        far_kernel,
        [dy_shape, act, act, (longer, BF), ((hidden_width, width // 2), BF)]
        + [((hidden_width // 4, width // 2), BF)] * 4,
        8, scalars, got_far, gate, up, d_hidden, dy_near, weights=(wg, wu, wd), downs=2,
        more=(pltpu.VMEM((hidden_width, width // 2), BF),),
    )
    home_far = over_ctx(back_far)

    quarter = lax.psum_scatter(
        partial, "dp", scatter_dimension=0, axis_index_groups=[[0, 2, 4, 6], [1, 3, 5, 7]], tiled=True
    )
    came = [swap(blocks[d], "dp", d << 1) for d in (1, 2, 3)]
    back_near = call(
        back_kernel, [(travel, BF)], 4, scalars, home, d_gate, d_up, weights=(wg, wu),
    )
    part, longer = ((256, 256), BF), ((272, 256), BF)
    *sums_far, leaving = call(
        first_kernel, [longer] * 4 + [(travel, BF)], 4, *table, home_far, back_near, after=came
    )
    home_near = over_ctx(leaving)
    came_far = [swap(sums_far[d], "tp", d) for d in (1, 2, 3)]
    end = ((96, width), BF)
    held, over = call(end_kernel, [end, end], 1, scalars, quarter, blocks[0], *came, after=(sums_far[0],))
    ends = swap(over, "dp", 1)
    total_far = call(total_kernel, [longer], 1, scalars, sums_far[0], *came_far, after=(over,))
    from_far = swap(total_far, "tp", 4)
    sums_near = call(
        functools.partial(combine_kernel, False), [part] * 4, 4, *table, home_near,
        after=(total_far,),
    )
    came_near = [swap(sums_near[d], "tp", d) for d in (1, 2, 3)]
    flat = ((128, 256), BF)
    combined, grad_tokens, lines = call(
        last_kernel, [flat, flat, (ids_t.shape, F32)], 1,
        scalars, total_far, from_far, sums_near[0], *came_near,
    )
    grad_down = call(add_kernel, [end], 2, scalars, held, ends)
    return combined, grad_tokens, lines.T, grad_down[None]


def solution(mesh):
    in_specs = (
        P(("dp", "ctx"), "tp"),
        P(("dp", "ctx"), "tp"),
        P(("dp", "ctx"), None),
        P(("dp", "ctx"), None),
        P(("ctx", "tp"), None, None),
        P(("ctx", "tp"), None, None),
        P(("ctx", "tp"), None, None),
    )
    out_specs = (
        P(("dp", "ctx"), "tp"),
        P(("dp", "ctx"), "tp"),
        P(("dp", "ctx"), None),
        P(("ctx", "tp"), "dp", None),
    )
    return jax.shard_map(shards, mesh=mesh, in_specs=in_specs, out_specs=out_specs, check_vma=False)
```

```python
import functools

import jax
import jax.numpy as jnp
from jax import lax
from jax.experimental import pallas as pl
from jax.experimental.pallas import tpu as pltpu
from jax.sharding import PartitionSpec as P

BF = jnp.bfloat16
F32 = jnp.float32
MAIN = 8
REST = 2
QUAD = 4
VMEM = 67_000_000
NEAR, FAR = (0, 1, 2, 4), (3, 5, 6, 7)
LAST, FIRST = (0, 1, 2, 3), (4, 5, 6, 7)


def iota(shape, dim):
    return lax.broadcasted_iota(jnp.int32, shape, dim)


def dot(a, b):
    return jnp.dot(a, b, preferred_element_type=F32)


def dot_nt(a, b):
    return lax.dot_general(a, b, (((1,), (1,)), ((), ())), preferred_element_type=F32)


def routing(ids_t, gates_t, lane):
    top, tokens = ids_t.shape
    rows = (MAIN + REST) * 16
    row = iota((rows, tokens), 0)
    left = row - MAIN * 16
    expert = jnp.where(left < 0, row >> 3, left >> 1) * 8 + lane
    slot = jnp.where(left < 0, row & 7, MAIN + (left & 1)).astype(F32)
    named = jnp.zeros((rows, tokens), F32)
    weight = jnp.zeros((rows, tokens), F32)
    for k in range(top):
        hit = ids_t[k : k + 1, :] == expert
        named = named + jnp.where(hit, 1.0, 0.0)
        weight = weight + jnp.where(hit, gates_t[k : k + 1, :], 0.0)
    before = jnp.where(iota((tokens, tokens), 0) < iota((tokens, tokens), 1), 1.0, 0.0)
    earlier = dot(named.astype(BF), before.astype(BF))
    holds = (named > 0.5) & (earlier == slot)
    return holds, weight, expert


def rest_mix():
    p, q = iota((256, 256), 0), iota((256, 256), 1)
    return jnp.where(q == ((p >> 1) & 7) * 32 + (p >> 4) * 2 + (p & 1), 1.0, 0.0).astype(BF)


def rest_unmix():
    q, p = iota((256, 256), 0), iota((256, 256), 1)
    return jnp.where(p == ((q >> 1) & 15) * 16 + (q >> 5) * 2 + (q & 1), 1.0, 0.0).astype(BF)


def fold(send_ref, shard, first, second):
    split = MAIN * 16
    tiles = [v[:split].reshape(16, MAIN, 256) for v in (first, second)]
    send_ref[:, shard * 16 : (shard + 1) * 16, :] = jnp.concatenate(tiles, axis=1).astype(BF)
    return [first[split:].astype(BF), second[split:].astype(BF)]


def fold_rest(send_ref, rest):
    mixed = dot(rest_mix(), jnp.concatenate(rest, axis=0))
    send_ref[:, QUAD * 16 : QUAD * 20, :] = mixed.reshape(16, 16, 256).astype(BF)


def unfold(recv_ref):
    tail = recv_ref[:, QUAD * 16 : QUAD * 20, :].astype(F32).reshape(256, 256).astype(BF)
    rest = dot(rest_unmix(), tail)
    out = []
    for shard in range(QUAD):
        both = recv_ref[:, shard * 16 : (shard + 1) * 16, :].astype(F32)
        pair = []
        for a in range(2):
            tiles = both[:, a * MAIN : (a + 1) * MAIN, :].reshape(MAIN * 16, 256)
            at = (shard * 2 + a) * 32
            pair.append(jnp.concatenate([tiles, rest[at : at + 32]], axis=0).astype(BF))
        out.append(pair)
    return out


def near_dispatch(where_ref, ids_ref, gates_ref, p0, p1, p2, p4, send_ref, pair_ref):
    dispatch(where_ref, ids_ref, gates_ref, (p0[...], p1[...], p2[...], p4[...]), send_ref)
    pair_ref[:256, :] = p0[...]
    pair_ref[256:, :] = p4[...]


def far_dispatch(where_ref, ids_ref, gates_ref, p37, p5, p6, send_ref):
    pieces = (p37[:256, :], p5[...], p6[...], p37[256:, :])
    dispatch(where_ref, ids_ref, gates_ref, pieces, send_ref)


def dispatch(where_ref, ids_ref, gates_ref, pieces, send_ref):
    holds, weight, _ = routing(ids_ref[...], gates_ref[...], where_ref[0])
    pick = jnp.where(holds, 1.0, 0.0).astype(BF)
    gain = jnp.sum(jnp.where(holds, weight, 0.0), axis=1, keepdims=True)
    rest = []
    for shard, piece in enumerate(pieces):
        x_rows = dot(pick, piece[:128, :])
        dy_rows = dot(pick, piece[128:, :]) * gain
        rest += fold(send_ref, shard, x_rows, dy_rows)
    fold_rest(send_ref, rest)


def shard_at(where_ref, offset):
    return pl.multiple_of((where_ref[0] ^ offset) * 256, 256)


def fetch(where_ref, wants, weights, held, sems):
    copies, waited = {}, set()
    for slot in range(max(len(v) for v in wants)):
        for n, offsets in enumerate(wants):
            if slot < len(offsets):
                at = pl.ds(shard_at(where_ref, offsets[slot]), 256)
                part = weights[n].at[:, at] if n == 2 else weights[n].at[at, :]
                copy = pltpu.make_async_copy(part, held[n].at[slot], sems.at[n, slot])
                copy.start()
                copies[n, offsets[slot]] = (copy, slot)

    def get(n, offset):
        copy, slot = copies[n, offset]
        if (n, offset) not in waited:
            copy.wait()
            waited.add((n, offset))
        return held[n][slot]

    return get


def inward(recv_ref, offsets, get, sums):
    gate, up, d_hidden = sums
    dys = []
    for offset, (x_rows, dy_rows) in zip(offsets, unfold(recv_ref)):
        dys.append(dy_rows)
        gate = gate + dot(x_rows, get(0, offset))
        up = up + dot(x_rows, get(1, offset))
        d_hidden = d_hidden + dot_nt(dy_rows, get(2, offset))
    return gate, up, d_hidden, dys


def outward(outs, d_gate, d_up, offsets, get, send_ref):
    rest = []
    for shard, offset in enumerate(offsets):
        dx = dot_nt(d_gate, get(0, offset)) + dot_nt(d_up, get(1, offset))
        rest += fold(send_ref, shard, outs[shard], dx)
    fold_rest(send_ref, rest)


def tail_pick(turn):
    p, q = (0, 1) if turn else (1, 0)
    shape = (128, 32) if turn else (32, 128)
    row, rest = iota(shape, p), iota(shape, q)
    return jnp.where(((row >> 3) == (rest >> 1)) & ((row & 7) == (rest & 1)), 1.0, 0.0).astype(BF)


def near_kernel(wants, where_ref, recv_ref, *refs):
    weights, held, sems = refs[:3], refs[7:10], refs[10]
    gate_ref, up_ref, dh_ref, dy_ref = refs[3:7]
    get = fetch(where_ref, wants, weights, held, sems)
    zero = jnp.zeros(gate_ref.shape, F32)
    gate_ref[...], up_ref[...], dh_ref[...], dys = inward(recv_ref, NEAR, get, (zero, zero, zero))
    for shard, rows in enumerate(dys):
        dy_ref[shard] = rows


def far_kernel(wants, where_ref, recv_ref, gate_ref, up_ref, dh_ref, near_ref, *refs):
    weights, outs, held, sems = refs[:3], refs[3:8], refs[8:11], refs[11]
    home_ref, dgate_ref, dup_ref, send_ref, partial_ref = outs
    get = fetch(where_ref, wants, weights, held, sems)
    gate, up, d_hidden, dys = inward(
        recv_ref, FAR, get, (gate_ref[...], up_ref[...], dh_ref[...])
    )
    s = jax.nn.sigmoid(gate)
    hidden32 = gate * s * up
    hidden = hidden32.astype(BF)
    d_gate = (d_hidden * up * s * (1.0 + gate * (1.0 - s))).astype(BF)
    d_up = (d_hidden * gate * s).astype(BF)
    dgate_ref[...] = d_gate
    dup_ref[...] = d_up
    dys = dict(zip(NEAR + FAR, [near_ref[shard] for shard in range(QUAD)] + dys))
    made = {offset: dot(hidden, get(2, offset)) for offset in FAR + NEAR}
    outward([made[offset] for offset in FIRST], d_gate, d_up, FIRST, get, send_ref)
    get(0, FAR[0]), get(1, FAR[0])
    for shard, offset in enumerate(LAST):
        home_ref[shard] = made[offset].astype(BF)
    dots = jnp.zeros((gate.shape[0], 1), F32)
    for offset in FAR + NEAR:
        terms = made[offset].astype(BF).astype(F32) * dys[offset].astype(F32)
        dots = dots + jnp.sum(terms, axis=1, keepdims=True)
    high = dots.astype(BF).astype(F32)
    terms = jnp.where(iota((dots.shape[0], 256), 1) < 128, high, dots - high)
    tail = dot(tail_pick(True), terms[MAIN * 16 :].astype(BF))
    terms = [v.reshape(16, 8, 256) for v in (terms[: MAIN * 16], tail)]
    send_ref[:, QUAD * 20 :, :] = jnp.concatenate(terms, axis=1).astype(BF)
    turned = hidden32.T.astype(BF)
    for n, offset in enumerate(NEAR + FAR):
        partial_ref[:, n * 256 : (n + 1) * 256] = dot(turned, dys[offset]).astype(BF)


def back_kernel(wants, where_ref, home_ref, dgate_ref, dup_ref, *refs):
    weights, send_ref, held, sems = refs[:2], refs[2], refs[3:5], refs[5]
    get = fetch(where_ref, wants, weights, held, sems)
    outs = [home_ref[shard].astype(F32) for shard in range(QUAD)]
    outward(outs, dgate_ref[...], dup_ref[...], LAST, get, send_ref)


def split_lines(lines):
    high = lines.astype(BF).astype(F32)
    middle = (lines - high).astype(BF).astype(F32)
    low = lines - high - middle
    pairs = [jnp.concatenate(v, axis=1) for v in ((high, middle), (low, jnp.zeros_like(low)))]
    return jnp.concatenate(pairs, axis=0).astype(BF)


def join_lines(ref):
    terms = ref[256:, :].astype(F32)
    return terms[:8, :128] + terms[:8, 128:] + terms[8:, :128]


def combine_kernel(first, where_ref, ids_ref, gates_ref, recv_ref, *outs):
    holds, weight, expert = routing(ids_ref[...], gates_ref[...], where_ref[0])
    gains = jnp.where(holds, weight, 0.0)
    picks = jnp.where(holds, 1.0, 0.0).T.astype(BF)
    turned = gains.T
    high = turned.astype(BF)
    low = (turned - high.astype(F32)).astype(BF)
    for (out, dx), to in zip(unfold(recv_ref), outs):
        to[:128, :] = (dot(high, out) + dot(low, out)).astype(BF)
        to[128:256, :] = dot(picks, dx).astype(BF)
    if not first:
        return
    terms = recv_ref[:, QUAD * 20 :, :].astype(F32)
    main, tail = [terms[:, n * 8 : (n + 1) * 8, :].reshape(128, 256) for n in range(2)]
    terms = jnp.concatenate([main, dot(tail_pick(False), tail.astype(BF))], axis=0)
    dots = terms[:, :1] + terms[:, 128:129]
    gain = jnp.sum(gains, axis=1, keepdims=True)
    slopes = jnp.where(gain > 0.0, dots / jnp.where(gain > 0.0, gain, 1.0), 0.0)
    sums = jnp.where(holds, slopes, 0.0)
    ids = ids_ref[...]
    lines = [
        jnp.sum(jnp.where(ids[k : k + 1, :] == expert, sums, 0.0), axis=0, keepdims=True)
        for k in range(ids.shape[0])
    ]
    lines = split_lines(jnp.concatenate(lines, axis=0))
    for to in outs:
        to[256:, :] = lines


def end_kernel(where_ref, sum_ref, held_ref, over_ref):
    for flip, ref in enumerate((held_ref, over_ref)):
        ref[...] = sum_ref[pl.ds(pl.multiple_of((where_ref[1] ^ flip) * 96, 96), 96), :]


def total_of(refs):
    total = refs[0][:256, :].astype(F32)
    for ref in refs[1:]:
        total = total + ref[:256, :].astype(F32)
    return total.astype(BF)


def total_kernel(where_ref, *refs):
    refs[-1][:256, :] = total_of(refs[:-1])
    lines = join_lines(refs[0])
    for ref in refs[1:-1]:
        lines = lines + join_lines(ref)
    refs[-1][256:, :] = split_lines(lines)


def last_kernel(where_ref, mine_ref, other_ref, *refs):
    total = total_of((other_ref, *refs[:-3]))
    refs[-3][...] = total[:128]
    refs[-2][...] = total[128:]
    refs[-1][...] = join_lines(mine_ref) + join_lines(other_ref)


def add_kernel(where_ref, held_ref, got_ref, out_ref):
    for n, offset in enumerate(NEAR + FAR):
        at = slice(n * 256, (n + 1) * 256)
        total = held_ref[:, at].astype(F32) + got_ref[:, at].astype(F32)
        out_ref[:, pl.ds(shard_at(where_ref, offset), 256)] = total.astype(BF)


def whole(shape):
    return pl.BlockSpec(shape, lambda i: (0,) * len(shape))


def call(kernel, outs, micros, scalars, *operands, weights=(), wants=(), after=()):
    specs = [pl.BlockSpec(memory_space=pltpu.SMEM)] + [whole(v.shape) for v in operands]
    specs += [pl.BlockSpec(memory_space=pl.ANY) for _ in (*weights, *after)]
    first = 1 + len(operands) + len(weights)
    last = first + len(after)

    def body(*refs):
        kernel(*refs[:first], *refs[last:])

    scratch = []
    if weights:
        wide = weights[0].shape[1]
        for n, offsets in enumerate(wants):
            cut = (wide, 256) if n == 2 else (256, wide)
            scratch.append(pltpu.VMEM((len(offsets), *cut), BF))
        scratch.append(pltpu.SemaphoreType.DMA((3, 2 * QUAD)))
        kernel = functools.partial(kernel, wants)
    shapes = [jax.ShapeDtypeStruct(s, d) for s, d in outs]
    results = pl.pallas_call(
        body,
        grid=(1,),
        out_shape=shapes,
        in_specs=specs,
        out_specs=[whole(v.shape) for v in shapes],
        scratch_shapes=scratch,
        compiler_params=pltpu.CompilerParams(vmem_limit_bytes=VMEM),
        cost_estimate=pl.CostEstimate(
            flops=micros * 10**9, bytes_accessed=micros * 3 * 10**6, transcendentals=0
        ),
    )(scalars, *operands, *weights, *after)
    return results[0] if len(results) == 1 else results


def swap(value, axis, bit):
    size = lax.axis_size(axis)
    return lax.ppermute(value, axis, [(i, i ^ bit) for i in range(size)])


def over_ctx(value):
    return lax.all_to_all(value, "ctx", split_axis=0, concat_axis=0, tiled=True)


def shards(tokens, grad_out, expert_ids, gate_weights, gate_proj, up_proj, down_proj):
    dp, lane = lax.axis_index("dp"), lax.axis_index("tp")
    scalars = jnp.stack([lane, dp & 1]).astype(jnp.int32)
    wg, wu, wd = gate_proj[0], up_proj[0], down_proj[0]
    width, hidden_width = wg.shape
    ids_t, gates_t = expert_ids.T, gate_weights.T
    table = (scalars, ids_t, gates_t)
    slots = (MAIN + REST) * 16
    travel = (16, QUAD * 20, 256)

    own = jnp.concatenate([tokens, grad_out], axis=0)
    near = {d: swap(own, "tp", d) for d in (4, 2, 1)}
    send_near, pair = call(
        near_dispatch, [(travel, BF), ((512, 256), BF)], 4, *table, own, near[1], near[2], near[4]
    )
    got_near = over_ctx(send_near)
    far = [swap(pair, "tp", 3), swap(near[4], "tp", 1), swap(near[4], "tp", 2)]
    send_far = call(far_dispatch, [(travel, BF)], 4, *table, *far, after=(send_near,))
    got_far = over_ctx(send_far)

    sums = ((slots, hidden_width), F32)
    dy_shape = ((QUAD, slots, 256), BF)
    act = ((slots, hidden_width), BF)
    gate, up, d_hidden, dy_near = call(
        near_kernel, [sums, sums, sums, dy_shape], 5, scalars, got_near,
        weights=(wg, wu, wd), wants=(NEAR,) * 3, after=(send_far,),
    )
    longer = (16, QUAD * 20 + 16, 256)
    home, d_gate, d_up, back_far, partial = call(
        far_kernel,
        [dy_shape, act, act, (longer, BF), ((hidden_width, width), BF)],
        8, scalars, got_far, gate, up, d_hidden, dy_near,
        weights=(wg, wu, wd), wants=(FAR + (4,), FAR + (4,), FAR + NEAR),
    )
    home_far = over_ctx(back_far)

    quarter = lax.psum_scatter(
        partial, "dp", scatter_dimension=0, axis_index_groups=[[0, 2, 4, 6], [1, 3, 5, 7]], tiled=True
    )
    back_near = call(
        back_kernel, [(travel, BF)], 4, scalars, home, d_gate, d_up,
        weights=(wg, wu), wants=(LAST, LAST),
    )
    home_near = over_ctx(back_near)

    part, longer = ((256, 256), BF), ((272, 256), BF)
    sums_far = call(
        functools.partial(combine_kernel, True), [longer] * 4, 4, *table, home_far,
        after=(back_near,),
    )
    came_far = [swap(sums_far[d], "tp", d) for d in (1, 2, 3)]
    end = ((96, width), BF)
    held, over = call(end_kernel, [end, end], 1, scalars, quarter, after=(sums_far[0],))
    ends = swap(over, "dp", 1)
    total_far = call(total_kernel, [longer], 1, scalars, sums_far[0], *came_far, after=(over,))
    from_far = swap(total_far, "tp", 4)
    sums_near = call(
        functools.partial(combine_kernel, False), [part] * 4, 4, *table, home_near,
        after=(total_far,),
    )
    came_near = [swap(sums_near[d], "tp", d) for d in (1, 2, 3)]
    flat = ((128, 256), BF)
    combined, grad_tokens, lines = call(
        last_kernel, [flat, flat, (ids_t.shape, F32)], 1,
        scalars, total_far, from_far, sums_near[0], *came_near,
    )
    grad_down = call(add_kernel, [end], 2, scalars, held, ends)
    return combined, grad_tokens, lines.T, grad_down[None]


def solution(mesh):
    in_specs = (
        P(("dp", "ctx"), "tp"),
        P(("dp", "ctx"), "tp"),
        P(("dp", "ctx"), None),
        P(("dp", "ctx"), None),
        P(("ctx", "tp"), None, None),
        P(("ctx", "tp"), None, None),
        P(("ctx", "tp"), None, None),
    )
    out_specs = (
        P(("dp", "ctx"), "tp"),
        P(("dp", "ctx"), "tp"),
        P(("dp", "ctx"), None),
        P(("ctx", "tp"), "dp", None),
    )
    return jax.shard_map(shards, mesh=mesh, in_specs=in_specs, out_specs=out_specs, check_vma=False)
```

```python
import functools

import jax
import jax.numpy as jnp
from jax import lax
from jax.experimental import pallas as pl
from jax.experimental.pallas import tpu as pltpu
from jax.sharding import PartitionSpec as P

BF = jnp.bfloat16
F32 = jnp.float32
MAIN = 8
REST = 2
QUAD = 4
VMEM = 67_000_000
NEAR, FAR = (0, 1, 2, 4), (3, 5, 6, 7)
LAST, FIRST = (0, 1, 2, 3), (4, 5, 6, 7)


def iota(shape, dim):
    return lax.broadcasted_iota(jnp.int32, shape, dim)


def dot(a, b):
    return jnp.dot(a, b, preferred_element_type=F32)


def dot_nt(a, b):
    return lax.dot_general(a, b, (((1,), (1,)), ((), ())), preferred_element_type=F32)


def routing(ids_t, gates_t, lane):
    top, tokens = ids_t.shape
    rows = (MAIN + REST) * 16
    row = iota((rows, tokens), 0)
    left = row - MAIN * 16
    expert = jnp.where(left < 0, row >> 3, left >> 1) * 8 + lane
    slot = jnp.where(left < 0, row & 7, MAIN + (left & 1)).astype(F32)
    named = jnp.zeros((rows, tokens), F32)
    weight = jnp.zeros((rows, tokens), F32)
    for k in range(top):
        hit = ids_t[k : k + 1, :] == expert
        named = named + jnp.where(hit, 1.0, 0.0)
        weight = weight + jnp.where(hit, gates_t[k : k + 1, :], 0.0)
    before = jnp.where(iota((tokens, tokens), 0) < iota((tokens, tokens), 1), 1.0, 0.0)
    earlier = dot(named.astype(BF), before.astype(BF))
    holds = (named > 0.5) & (earlier == slot)
    return holds, weight, expert


def rest_mix():
    p, q = iota((256, 256), 0), iota((256, 256), 1)
    return jnp.where(q == ((p >> 1) & 7) * 32 + (p >> 4) * 2 + (p & 1), 1.0, 0.0).astype(BF)


def rest_unmix():
    q, p = iota((256, 256), 0), iota((256, 256), 1)
    return jnp.where(p == ((q >> 1) & 15) * 16 + (q >> 5) * 2 + (q & 1), 1.0, 0.0).astype(BF)


def fold(send_ref, shard, first, second):
    split = MAIN * 16
    tiles = [v[:split].reshape(16, MAIN, 256) for v in (first, second)]
    send_ref[:, shard * 16 : (shard + 1) * 16, :] = jnp.concatenate(tiles, axis=1).astype(BF)
    return [first[split:].astype(BF), second[split:].astype(BF)]


def fold_rest(send_ref, rest):
    mixed = dot(rest_mix(), jnp.concatenate(rest, axis=0))
    send_ref[:, QUAD * 16 : QUAD * 20, :] = mixed.reshape(16, 16, 256).astype(BF)


def unfold(recv_ref):
    tail = recv_ref[:, QUAD * 16 : QUAD * 20, :].astype(F32).reshape(256, 256).astype(BF)
    rest = dot(rest_unmix(), tail)
    out = []
    for shard in range(QUAD):
        both = recv_ref[:, shard * 16 : (shard + 1) * 16, :].astype(F32)
        pair = []
        for a in range(2):
            tiles = both[:, a * MAIN : (a + 1) * MAIN, :].reshape(MAIN * 16, 256)
            at = (shard * 2 + a) * 32
            pair.append(jnp.concatenate([tiles, rest[at : at + 32]], axis=0).astype(BF))
        out.append(pair)
    return out


def near_dispatch(where_ref, ids_ref, gates_ref, p0, p1, p2, p4, send_ref, pair_ref):
    dispatch(where_ref, ids_ref, gates_ref, (p0[...], p1[...], p2[...], p4[...]), send_ref)
    pair_ref[:256, :] = p0[...]
    pair_ref[256:, :] = p4[...]


def far_dispatch(where_ref, ids_ref, gates_ref, p37, p5, p6, send_ref):
    pieces = (p37[:256, :], p5[...], p6[...], p37[256:, :])
    dispatch(where_ref, ids_ref, gates_ref, pieces, send_ref)


def dispatch(where_ref, ids_ref, gates_ref, pieces, send_ref):
    holds, weight, _ = routing(ids_ref[...], gates_ref[...], where_ref[0])
    pick = jnp.where(holds, 1.0, 0.0).astype(BF)
    gain = jnp.sum(jnp.where(holds, weight, 0.0), axis=1, keepdims=True)
    rest = []
    for shard, piece in enumerate(pieces):
        x_rows = dot(pick, piece[:128, :])
        dy_rows = dot(pick, piece[128:, :]) * gain
        rest += fold(send_ref, shard, x_rows, dy_rows)
    fold_rest(send_ref, rest)


def shard_at(where_ref, offset):
    return pl.multiple_of((where_ref[0] ^ offset) * 256, 256)


def fetch(where_ref, wants, weights, held, sems):
    copies, waited = {}, set()
    for slot in range(max(len(v) for v in wants)):
        for n, offsets in enumerate(wants):
            if slot < len(offsets):
                at = pl.ds(shard_at(where_ref, offsets[slot]), 256)
                part = weights[n].at[:, at] if n == 2 else weights[n].at[at, :]
                copy = pltpu.make_async_copy(part, held[n].at[slot], sems.at[n, slot])
                copy.start()
                copies[n, offsets[slot]] = (copy, slot)

    def get(n, offset):
        copy, slot = copies[n, offset]
        if (n, offset) not in waited:
            copy.wait()
            waited.add((n, offset))
        return held[n][slot]

    return get


def inward(recv_ref, offsets, get, sums):
    gate, up, d_hidden = sums
    dys = []
    for offset, (x_rows, dy_rows) in zip(offsets, unfold(recv_ref)):
        dys.append(dy_rows)
        gate = gate + dot(x_rows, get(0, offset))
        up = up + dot(x_rows, get(1, offset))
        d_hidden = d_hidden + dot_nt(dy_rows, get(2, offset))
    return gate, up, d_hidden, dys


def outward(outs, d_gate, d_up, offsets, get, send_ref):
    rest = []
    for shard, offset in enumerate(offsets):
        dx = dot_nt(d_gate, get(0, offset)) + dot_nt(d_up, get(1, offset))
        rest += fold(send_ref, shard, outs[shard], dx)
    fold_rest(send_ref, rest)


def tail_pick(turn):
    p, q = (0, 1) if turn else (1, 0)
    shape = (128, 32) if turn else (32, 128)
    row, rest = iota(shape, p), iota(shape, q)
    return jnp.where(((row >> 3) == (rest >> 1)) & ((row & 7) == (rest & 1)), 1.0, 0.0).astype(BF)


def near_kernel(wants, where_ref, recv_ref, *refs):
    weights, held, sems = refs[:3], refs[7:10], refs[10]
    gate_ref, up_ref, dh_ref, dy_ref = refs[3:7]
    get = fetch(where_ref, wants, weights, held, sems)
    zero = jnp.zeros(gate_ref.shape, F32)
    gate_ref[...], up_ref[...], dh_ref[...], dys = inward(recv_ref, NEAR, get, (zero, zero, zero))
    for shard, rows in enumerate(dys):
        dy_ref[shard] = rows


def far_kernel(wants, where_ref, recv_ref, gate_ref, up_ref, dh_ref, near_ref, *refs):
    weights, outs, held, sems, block, ends = refs[:3], refs[3:8], refs[8:11], *refs[11:14]
    home_ref, dgate_ref, dup_ref, send_ref, partial_ref = outs
    get = fetch(where_ref, wants, weights, held, sems)
    gate, up, d_hidden, dys = inward(
        recv_ref, FAR, get, (gate_ref[...], up_ref[...], dh_ref[...])
    )
    s = jax.nn.sigmoid(gate)
    hidden32 = gate * s * up
    hidden = hidden32.astype(BF)
    d_gate = (d_hidden * up * s * (1.0 + gate * (1.0 - s))).astype(BF)
    d_up = (d_hidden * gate * s).astype(BF)
    dgate_ref[...] = d_gate
    dup_ref[...] = d_up
    dys = dict(zip(NEAR + FAR, [near_ref[shard] for shard in range(QUAD)] + dys))
    turned = hidden32.T.astype(BF)
    leaving = []
    for n, offset in enumerate(NEAR + FAR):
        at = slice(n * 256, (n + 1) * 256)
        block[:, at] = dot(turned, dys[offset]).astype(BF)
        copy = pltpu.make_async_copy(block.at[:, at], partial_ref.at[:, at], ends.at[n])
        copy.start()
        leaving.append(copy)
    made = {offset: dot(hidden, get(2, offset)) for offset in FAR + NEAR}
    outward([made[offset] for offset in FIRST], d_gate, d_up, FIRST, get, send_ref)
    get(0, FAR[0]), get(1, FAR[0])
    for shard, offset in enumerate(LAST):
        home_ref[shard] = made[offset].astype(BF)
    dots = jnp.zeros((gate.shape[0], 1), F32)
    for offset in FAR + NEAR:
        terms = made[offset].astype(BF).astype(F32) * dys[offset].astype(F32)
        dots = dots + jnp.sum(terms, axis=1, keepdims=True)
    high = dots.astype(BF).astype(F32)
    terms = jnp.where(iota((dots.shape[0], 256), 1) < 128, high, dots - high)
    tail = dot(tail_pick(True), terms[MAIN * 16 :].astype(BF))
    terms = [v.reshape(16, 8, 256) for v in (terms[: MAIN * 16], tail)]
    send_ref[:, QUAD * 20 :, :] = jnp.concatenate(terms, axis=1).astype(BF)
    for copy in leaving:
        copy.wait()


def back_kernel(wants, where_ref, home_ref, dgate_ref, dup_ref, *refs):
    weights, send_ref, held, sems = refs[:2], refs[2], refs[3:5], refs[5]
    get = fetch(where_ref, wants, weights, held, sems)
    outs = [home_ref[shard].astype(F32) for shard in range(QUAD)]
    outward(outs, dgate_ref[...], dup_ref[...], LAST, get, send_ref)


def split_lines(lines):
    high = lines.astype(BF).astype(F32)
    middle = (lines - high).astype(BF).astype(F32)
    low = lines - high - middle
    pairs = [jnp.concatenate(v, axis=1) for v in ((high, middle), (low, jnp.zeros_like(low)))]
    return jnp.concatenate(pairs, axis=0).astype(BF)


def join_lines(ref):
    terms = ref[256:, :].astype(F32)
    return terms[:8, :128] + terms[:8, 128:] + terms[8:, :128]


def combine_kernel(first, where_ref, ids_ref, gates_ref, recv_ref, *outs):
    holds, weight, expert = routing(ids_ref[...], gates_ref[...], where_ref[0])
    gains = jnp.where(holds, weight, 0.0)
    picks = jnp.where(holds, 1.0, 0.0).T.astype(BF)
    turned = gains.T
    high = turned.astype(BF)
    low = (turned - high.astype(F32)).astype(BF)
    for (out, dx), to in zip(unfold(recv_ref), outs):
        to[:128, :] = (dot(high, out) + dot(low, out)).astype(BF)
        to[128:256, :] = dot(picks, dx).astype(BF)
    if not first:
        return
    terms = recv_ref[:, QUAD * 20 :, :].astype(F32)
    main, tail = [terms[:, n * 8 : (n + 1) * 8, :].reshape(128, 256) for n in range(2)]
    terms = jnp.concatenate([main, dot(tail_pick(False), tail.astype(BF))], axis=0)
    dots = terms[:, :1] + terms[:, 128:129]
    gain = jnp.sum(gains, axis=1, keepdims=True)
    slopes = jnp.where(gain > 0.0, dots / jnp.where(gain > 0.0, gain, 1.0), 0.0)
    sums = jnp.where(holds, slopes, 0.0)
    ids = ids_ref[...]
    lines = [
        jnp.sum(jnp.where(ids[k : k + 1, :] == expert, sums, 0.0), axis=0, keepdims=True)
        for k in range(ids.shape[0])
    ]
    lines = split_lines(jnp.concatenate(lines, axis=0))
    for to in outs:
        to[256:, :] = lines


def end_kernel(where_ref, sum_ref, over_ref):
    over_ref[...] = sum_ref[pl.ds(pl.multiple_of((where_ref[1] ^ 1) * 96, 96), 96), :]


def total_of(refs):
    total = refs[0][:256, :].astype(F32)
    for ref in refs[1:]:
        total = total + ref[:256, :].astype(F32)
    return total.astype(BF)


def total_kernel(where_ref, *refs):
    refs[-1][:256, :] = total_of(refs[:-1])
    lines = join_lines(refs[0])
    for ref in refs[1:-1]:
        lines = lines + join_lines(ref)
    refs[-1][256:, :] = split_lines(lines)


def last_kernel(where_ref, mine_ref, other_ref, sum_ref, got_ref, *refs):
    combined_ref, grad_ref, lines_ref, down_ref = refs[-4:]
    total = total_of((other_ref, *refs[:-4]))
    combined_ref[...] = total[:128]
    grad_ref[...] = total[128:]
    lines_ref[...] = join_lines(mine_ref) + join_lines(other_ref)
    rows = pl.ds(pl.multiple_of(where_ref[1] * 96, 96), 96)
    for n, offset in enumerate(NEAR + FAR):
        at = slice(n * 256, (n + 1) * 256)
        total = sum_ref[rows, at].astype(F32) + got_ref[:, at].astype(F32)
        down_ref[:, pl.ds(shard_at(where_ref, offset), 256)] = total.astype(BF)


def whole(shape):
    return pl.BlockSpec(shape, lambda i: (0,) * len(shape))


def call(kernel, outs, micros, scalars, *operands, weights=(), wants=(), more=(), loose=0, after=()):
    specs = [pl.BlockSpec(memory_space=pltpu.SMEM)] + [whole(v.shape) for v in operands]
    specs += [pl.BlockSpec(memory_space=pl.ANY) for _ in (*weights, *after)]
    first = 1 + len(operands) + len(weights)
    last = first + len(after)

    def body(*refs):
        kernel(*refs[:first], *refs[last:])

    scratch = []
    if weights:
        wide = weights[0].shape[1]
        for n, offsets in enumerate(wants):
            cut = (wide, 256) if n == 2 else (256, wide)
            scratch.append(pltpu.VMEM((len(offsets), *cut), BF))
        scratch.append(pltpu.SemaphoreType.DMA((3, 2 * QUAD)))
        kernel = functools.partial(kernel, wants)
    shapes = [jax.ShapeDtypeStruct(s, d) for s, d in outs]
    results = pl.pallas_call(
        body,
        grid=(1,),
        out_shape=shapes,
        in_specs=specs,
        out_specs=[whole(v.shape) for v in shapes[: len(shapes) - loose]]
        + [pl.BlockSpec(memory_space=pl.ANY)] * loose,
        scratch_shapes=[*scratch, *more],
        compiler_params=pltpu.CompilerParams(vmem_limit_bytes=VMEM),
        cost_estimate=pl.CostEstimate(
            flops=micros * 10**9, bytes_accessed=micros * 3 * 10**6, transcendentals=0
        ),
    )(scalars, *operands, *weights, *after)
    return results[0] if len(results) == 1 else results


def swap(value, axis, bit):
    size = lax.axis_size(axis)
    return lax.ppermute(value, axis, [(i, i ^ bit) for i in range(size)])


def over_ctx(value):
    return lax.all_to_all(value, "ctx", split_axis=0, concat_axis=0, tiled=True)


def shards(tokens, grad_out, expert_ids, gate_weights, gate_proj, up_proj, down_proj):
    dp, lane = lax.axis_index("dp"), lax.axis_index("tp")
    scalars = jnp.stack([lane, dp & 1]).astype(jnp.int32)
    wg, wu, wd = gate_proj[0], up_proj[0], down_proj[0]
    width, hidden_width = wg.shape
    ids_t, gates_t = expert_ids.T, gate_weights.T
    table = (scalars, ids_t, gates_t)
    slots = (MAIN + REST) * 16
    travel = (16, QUAD * 20, 256)

    own = jnp.concatenate([tokens, grad_out], axis=0)
    near = {d: swap(own, "tp", d) for d in (4, 2, 1)}
    send_near, pair = call(
        near_dispatch, [(travel, BF), ((512, 256), BF)], 4, *table, own, near[1], near[2], near[4]
    )
    got_near = over_ctx(send_near)
    far = [swap(pair, "tp", 3), swap(near[4], "tp", 1), swap(near[4], "tp", 2)]
    send_far = call(far_dispatch, [(travel, BF)], 4, *table, *far, after=(send_near,))
    got_far = over_ctx(send_far)

    sums = ((slots, hidden_width), F32)
    dy_shape = ((QUAD, slots, 256), BF)
    act = ((slots, hidden_width), BF)
    gate, up, d_hidden, dy_near = call(
        near_kernel, [sums, sums, sums, dy_shape], 5, scalars, got_near,
        weights=(wg, wu, wd), wants=(NEAR,) * 3, after=(send_far,),
    )
    longer = (16, QUAD * 20 + 16, 256)
    home, d_gate, d_up, back_far, partial = call(
        far_kernel,
        [dy_shape, act, act, (longer, BF), ((hidden_width, width), BF)],
        8, scalars, got_far, gate, up, d_hidden, dy_near,
        weights=(wg, wu, wd), wants=(FAR + (4,), FAR + (4,), FAR + NEAR),
        more=(pltpu.VMEM((hidden_width, width), BF), pltpu.SemaphoreType.DMA((2 * QUAD,))),
        loose=1,
    )
    home_far = over_ctx(back_far)

    quarter = lax.psum_scatter(
        partial, "dp", scatter_dimension=0, axis_index_groups=[[0, 2, 4, 6], [1, 3, 5, 7]], tiled=True
    )
    back_near = call(
        back_kernel, [(travel, BF)], 4, scalars, home, d_gate, d_up,
        weights=(wg, wu), wants=(LAST, LAST),
    )
    home_near = over_ctx(back_near)

    part, longer = ((256, 256), BF), ((272, 256), BF)
    sums_far = call(
        functools.partial(combine_kernel, True), [longer] * 4, 4, *table, home_far,
        after=(back_near,),
    )
    came_far = [swap(sums_far[d], "tp", d) for d in (1, 2, 3)]
    end = ((96, width), BF)
    over = call(end_kernel, [end], 1, scalars, quarter, after=(sums_far[0],))
    ends = swap(over, "dp", 1)
    total_far = call(total_kernel, [longer], 1, scalars, sums_far[0], *came_far, after=(over,))
    from_far = swap(total_far, "tp", 4)
    sums_near = call(
        functools.partial(combine_kernel, False), [part] * 4, 4, *table, home_near,
        after=(total_far,),
    )
    came_near = [swap(sums_near[d], "tp", d) for d in (1, 2, 3)]
    flat = ((128, 256), BF)
    combined, grad_tokens, lines, grad_down = call(
        last_kernel, [flat, flat, (ids_t.shape, F32), end], 2,
        scalars, total_far, from_far, quarter, ends, sums_near[0], *came_near,
    )
    return combined, grad_tokens, lines.T, grad_down[None]


def solution(mesh):
    in_specs = (
        P(("dp", "ctx"), "tp"),
        P(("dp", "ctx"), "tp"),
        P(("dp", "ctx"), None),
        P(("dp", "ctx"), None),
        P(("ctx", "tp"), None, None),
        P(("ctx", "tp"), None, None),
        P(("ctx", "tp"), None, None),
    )
    out_specs = (
        P(("dp", "ctx"), "tp"),
        P(("dp", "ctx"), "tp"),
        P(("dp", "ctx"), None),
        P(("ctx", "tp"), "dp", None),
    )
    return jax.shard_map(shards, mesh=mesh, in_specs=in_specs, out_specs=out_specs, check_vma=False)
```

```python
import functools

import jax
import jax.numpy as jnp
from jax import lax
from jax.experimental import pallas as pl
from jax.experimental.pallas import tpu as pltpu
from jax.sharding import PartitionSpec as P

BF = jnp.bfloat16
F32 = jnp.float32
MAIN = 8
REST = 2
QUAD = 4
VMEM = 67_000_000
NEAR, FAR = (0, 1, 2, 4), (3, 5, 6, 7)
LAST, FIRST = (0, 1, 2, 3), (4, 5, 6, 7)


def iota(shape, dim):
    return lax.broadcasted_iota(jnp.int32, shape, dim)


def dot(a, b):
    return jnp.dot(a, b, preferred_element_type=F32)


def dot_nt(a, b):
    return lax.dot_general(a, b, (((1,), (1,)), ((), ())), preferred_element_type=F32)


def routing(ids_t, gates_t, lane):
    top, tokens = ids_t.shape
    rows = (MAIN + REST) * 16
    row = iota((rows, tokens), 0)
    left = row - MAIN * 16
    expert = jnp.where(left < 0, row >> 3, left >> 1) * 8 + lane
    slot = jnp.where(left < 0, row & 7, MAIN + (left & 1)).astype(F32)
    named = jnp.zeros((rows, tokens), F32)
    weight = jnp.zeros((rows, tokens), F32)
    for k in range(top):
        hit = ids_t[k : k + 1, :] == expert
        named = named + jnp.where(hit, 1.0, 0.0)
        weight = weight + jnp.where(hit, gates_t[k : k + 1, :], 0.0)
    before = jnp.where(iota((tokens, tokens), 0) < iota((tokens, tokens), 1), 1.0, 0.0)
    earlier = dot(named.astype(BF), before.astype(BF))
    holds = (named > 0.5) & (earlier == slot)
    return holds, weight, expert


def rest_mix():
    p, q = iota((256, 256), 0), iota((256, 256), 1)
    return jnp.where(q == ((p >> 1) & 7) * 32 + (p >> 4) * 2 + (p & 1), 1.0, 0.0).astype(BF)


def rest_unmix():
    q, p = iota((256, 256), 0), iota((256, 256), 1)
    return jnp.where(p == ((q >> 1) & 15) * 16 + (q >> 5) * 2 + (q & 1), 1.0, 0.0).astype(BF)


def fold(send_ref, shard, first, second):
    split = MAIN * 16
    tiles = [v[:split].reshape(16, MAIN, 256) for v in (first, second)]
    send_ref[:, shard * 16 : (shard + 1) * 16, :] = jnp.concatenate(tiles, axis=1).astype(BF)
    return [first[split:].astype(BF), second[split:].astype(BF)]


def fold_rest(send_ref, rest):
    mixed = dot(rest_mix(), jnp.concatenate(rest, axis=0))
    send_ref[:, QUAD * 16 : QUAD * 20, :] = mixed.reshape(16, 16, 256).astype(BF)


def unfold(recv_ref):
    tail = recv_ref[:, QUAD * 16 : QUAD * 20, :].astype(F32).reshape(256, 256).astype(BF)
    rest = dot(rest_unmix(), tail)
    out = []
    for shard in range(QUAD):
        both = recv_ref[:, shard * 16 : (shard + 1) * 16, :].astype(F32)
        pair = []
        for a in range(2):
            tiles = both[:, a * MAIN : (a + 1) * MAIN, :].reshape(MAIN * 16, 256)
            at = (shard * 2 + a) * 32
            pair.append(jnp.concatenate([tiles, rest[at : at + 32]], axis=0).astype(BF))
        out.append(pair)
    return out


def near_dispatch(where_ref, ids_ref, gates_ref, p0, p1, p2, p4, send_ref, pair_ref):
    dispatch(where_ref, ids_ref, gates_ref, (p0[...], p1[...], p2[...], p4[...]), send_ref)
    pair_ref[:256, :] = p0[...]
    pair_ref[256:, :] = p4[...]


def far_dispatch(where_ref, ids_ref, gates_ref, p37, p5, p6, send_ref):
    pieces = (p37[:256, :], p5[...], p6[...], p37[256:, :])
    dispatch(where_ref, ids_ref, gates_ref, pieces, send_ref)


def dispatch(where_ref, ids_ref, gates_ref, pieces, send_ref):
    holds, weight, _ = routing(ids_ref[...], gates_ref[...], where_ref[0])
    pick = jnp.where(holds, 1.0, 0.0).astype(BF)
    gain = jnp.sum(jnp.where(holds, weight, 0.0), axis=1, keepdims=True)
    rest = []
    for shard, piece in enumerate(pieces):
        x_rows = dot(pick, piece[:128, :])
        dy_rows = dot(pick, piece[128:, :]) * gain
        rest += fold(send_ref, shard, x_rows, dy_rows)
    fold_rest(send_ref, rest)


def shard_at(where_ref, offset):
    return pl.multiple_of((where_ref[0] ^ offset) * 256, 256)


def fetch(where_ref, wants, weights, held, sems):
    copies, waited = {}, set()
    for slot in range(max(len(v) for v in wants)):
        for n, offsets in enumerate(wants):
            if slot < len(offsets):
                at = pl.ds(shard_at(where_ref, offsets[slot]), 256)
                part = weights[n].at[:, at] if n == 2 else weights[n].at[at, :]
                copy = pltpu.make_async_copy(part, held[n].at[slot], sems.at[n, slot])
                copy.start()
                copies[n, offsets[slot]] = (copy, slot)

    def get(n, offset):
        copy, slot = copies[n, offset]
        if (n, offset) not in waited:
            copy.wait()
            waited.add((n, offset))
        return held[n][slot]

    return get


def inward(recv_ref, offsets, get, sums):
    gate, up, d_hidden = sums
    dys = []
    for offset, (x_rows, dy_rows) in zip(offsets, unfold(recv_ref)):
        dys.append(dy_rows)
        gate = gate + dot(x_rows, get(0, offset))
        up = up + dot(x_rows, get(1, offset))
        d_hidden = d_hidden + dot_nt(dy_rows, get(2, offset))
    return gate, up, d_hidden, dys


def outward(hidden, d_gate, d_up, offsets, get, send_ref):
    rest = []
    for shard, offset in enumerate(offsets):
        out = dot(hidden, get(2, offset))
        dx = dot_nt(d_gate, get(0, offset)) + dot_nt(d_up, get(1, offset))
        rest += fold(send_ref, shard, out, dx)
    fold_rest(send_ref, rest)


def tail_pick(turn):
    p, q = (0, 1) if turn else (1, 0)
    shape = (128, 32) if turn else (32, 128)
    row, rest = iota(shape, p), iota(shape, q)
    return jnp.where(((row >> 3) == (rest >> 1)) & ((row & 7) == (rest & 1)), 1.0, 0.0).astype(BF)


def near_kernel(wants, where_ref, recv_ref, *refs):
    weights, held, sems = refs[:3], refs[7:10], refs[10]
    gate_ref, up_ref, dh_ref, dy_ref = refs[3:7]
    get = fetch(where_ref, wants, weights, held, sems)
    zero = jnp.zeros(gate_ref.shape, F32)
    gate_ref[...], up_ref[...], dh_ref[...], dys = inward(recv_ref, NEAR, get, (zero, zero, zero))
    for shard, rows in enumerate(dys):
        dy_ref[shard] = rows


def far_kernel(wants, where_ref, recv_ref, gate_ref, up_ref, dh_ref, near_ref, *refs):
    weights, outs, held, sems, block, ends = refs[:3], refs[3:8], refs[8:11], *refs[11:14]
    hidden_ref, dgate_ref, dup_ref, send_ref, partial_ref = outs
    get = fetch(where_ref, wants, weights, held, sems)
    gate, up, d_hidden, dys = inward(
        recv_ref, FAR, get, (gate_ref[...], up_ref[...], dh_ref[...])
    )
    s = jax.nn.sigmoid(gate)
    hidden32 = gate * s * up
    hidden = hidden32.astype(BF)
    d_gate = (d_hidden * up * s * (1.0 + gate * (1.0 - s))).astype(BF)
    d_up = (d_hidden * gate * s).astype(BF)
    hidden_ref[...] = hidden
    dgate_ref[...] = d_gate
    dup_ref[...] = d_up
    dys = dict(zip(NEAR + FAR, [near_ref[shard] for shard in range(QUAD)] + dys))
    turned = hidden32.T.astype(BF)
    leaving = []
    for n, offset in enumerate(NEAR + FAR):
        at = slice(n * 256, (n + 1) * 256)
        block[:, at] = dot(turned, dys[offset]).astype(BF)
        copy = pltpu.make_async_copy(block.at[:, at], partial_ref.at[:, at], ends.at[n])
        copy.start()
        leaving.append(copy)
    outward(hidden, d_gate, d_up, FIRST, get, send_ref)
    dots = jnp.sum(hidden.astype(F32) * d_hidden, axis=1, keepdims=True)
    high = dots.astype(BF).astype(F32)
    terms = jnp.where(iota((dots.shape[0], 256), 1) < 128, high, dots - high)
    tail = dot(tail_pick(True), terms[MAIN * 16 :].astype(BF))
    terms = [v.reshape(16, 8, 256) for v in (terms[: MAIN * 16], tail)]
    send_ref[:, QUAD * 20 :, :] = jnp.concatenate(terms, axis=1).astype(BF)
    for copy in leaving:
        copy.wait()


def back_kernel(wants, where_ref, hidden_ref, dgate_ref, dup_ref, *refs):
    weights, send_ref, held, sems = refs[:3], refs[3], refs[4:7], refs[7]
    get = fetch(where_ref, wants, weights, held, sems)
    outward(hidden_ref[...], dgate_ref[...], dup_ref[...], LAST, get, send_ref)


def split_lines(lines):
    high = lines.astype(BF).astype(F32)
    middle = (lines - high).astype(BF).astype(F32)
    low = lines - high - middle
    pairs = [jnp.concatenate(v, axis=1) for v in ((high, middle), (low, jnp.zeros_like(low)))]
    return jnp.concatenate(pairs, axis=0).astype(BF)


def join_lines(ref):
    terms = ref[256:, :].astype(F32)
    return terms[:8, :128] + terms[:8, 128:] + terms[8:, :128]


def combine_kernel(first, where_ref, ids_ref, gates_ref, recv_ref, *outs):
    holds, weight, expert = routing(ids_ref[...], gates_ref[...], where_ref[0])
    gains = jnp.where(holds, weight, 0.0)
    picks = jnp.where(holds, 1.0, 0.0).T.astype(BF)
    turned = gains.T
    high = turned.astype(BF)
    low = (turned - high.astype(F32)).astype(BF)
    for (out, dx), to in zip(unfold(recv_ref), outs):
        to[:128, :] = (dot(high, out) + dot(low, out)).astype(BF)
        to[128:256, :] = dot(picks, dx).astype(BF)
    if not first:
        return
    terms = recv_ref[:, QUAD * 20 :, :].astype(F32)
    main, tail = [terms[:, n * 8 : (n + 1) * 8, :].reshape(128, 256) for n in range(2)]
    terms = jnp.concatenate([main, dot(tail_pick(False), tail.astype(BF))], axis=0)
    dots = terms[:, :1] + terms[:, 128:129]
    gain = jnp.sum(gains, axis=1, keepdims=True)
    slopes = jnp.where(gain > 0.0, dots / jnp.where(gain > 0.0, gain, 1.0), 0.0)
    sums = jnp.where(holds, slopes, 0.0)
    ids = ids_ref[...]
    lines = [
        jnp.sum(jnp.where(ids[k : k + 1, :] == expert, sums, 0.0), axis=0, keepdims=True)
        for k in range(ids.shape[0])
    ]
    lines = split_lines(jnp.concatenate(lines, axis=0))
    for to in outs:
        to[256:, :] = lines


def end_kernel(where_ref, sum_ref, over_ref):
    over_ref[...] = sum_ref[pl.ds(pl.multiple_of((where_ref[1] ^ 1) * 96, 96), 96), :]


def total_of(refs):
    total = refs[0][:256, :].astype(F32)
    for ref in refs[1:]:
        total = total + ref[:256, :].astype(F32)
    return total.astype(BF)


def total_kernel(where_ref, *refs):
    refs[-1][:256, :] = total_of(refs[:-1])
    lines = join_lines(refs[0])
    for ref in refs[1:-1]:
        lines = lines + join_lines(ref)
    refs[-1][256:, :] = split_lines(lines)


def last_kernel(where_ref, mine_ref, other_ref, sum_ref, got_ref, *refs):
    combined_ref, grad_ref, lines_ref, down_ref = refs[-4:]
    total = total_of((other_ref, *refs[:-4]))
    combined_ref[...] = total[:128]
    grad_ref[...] = total[128:]
    lines_ref[...] = join_lines(mine_ref) + join_lines(other_ref)
    rows = pl.ds(pl.multiple_of(where_ref[1] * 96, 96), 96)
    for n, offset in enumerate(NEAR + FAR):
        at = slice(n * 256, (n + 1) * 256)
        total = sum_ref[rows, at].astype(F32) + got_ref[:, at].astype(F32)
        down_ref[:, pl.ds(shard_at(where_ref, offset), 256)] = total.astype(BF)


def whole(shape):
    return pl.BlockSpec(shape, lambda i: (0,) * len(shape))


def call(kernel, outs, micros, scalars, *operands, weights=(), wants=(), more=(), loose=0, after=()):
    specs = [pl.BlockSpec(memory_space=pltpu.SMEM)] + [whole(v.shape) for v in operands]
    specs += [pl.BlockSpec(memory_space=pl.ANY) for _ in (*weights, *after)]
    first = 1 + len(operands) + len(weights)
    last = first + len(after)

    def body(*refs):
        kernel(*refs[:first], *refs[last:])

    scratch = []
    if weights:
        wide = weights[0].shape[1]
        for n, offsets in enumerate(wants):
            cut = (wide, 256) if n == 2 else (256, wide)
            scratch.append(pltpu.VMEM((len(offsets), *cut), BF))
        scratch.append(pltpu.SemaphoreType.DMA((3, 2 * QUAD)))
        kernel = functools.partial(kernel, wants)
    shapes = [jax.ShapeDtypeStruct(s, d) for s, d in outs]
    results = pl.pallas_call(
        body,
        grid=(1,),
        out_shape=shapes,
        in_specs=specs,
        out_specs=[whole(v.shape) for v in shapes[: len(shapes) - loose]]
        + [pl.BlockSpec(memory_space=pl.ANY)] * loose,
        scratch_shapes=[*scratch, *more],
        compiler_params=pltpu.CompilerParams(vmem_limit_bytes=VMEM),
        cost_estimate=pl.CostEstimate(
            flops=micros * 10**9, bytes_accessed=micros * 3 * 10**6, transcendentals=0
        ),
    )(scalars, *operands, *weights, *after)
    return results[0] if len(results) == 1 else results


def swap(value, axis, bit):
    size = lax.axis_size(axis)
    return lax.ppermute(value, axis, [(i, i ^ bit) for i in range(size)])


def over_ctx(value):
    return lax.all_to_all(value, "ctx", split_axis=0, concat_axis=0, tiled=True)


def shards(tokens, grad_out, expert_ids, gate_weights, gate_proj, up_proj, down_proj):
    dp, lane = lax.axis_index("dp"), lax.axis_index("tp")
    scalars = jnp.stack([lane, dp & 1]).astype(jnp.int32)
    wg, wu, wd = gate_proj[0], up_proj[0], down_proj[0]
    width, hidden_width = wg.shape
    ids_t, gates_t = expert_ids.T, gate_weights.T
    table = (scalars, ids_t, gates_t)
    slots = (MAIN + REST) * 16
    travel = (16, QUAD * 20, 256)

    own = jnp.concatenate([tokens, grad_out], axis=0)
    near = {d: swap(own, "tp", d) for d in (4, 2, 1)}
    send_near, pair = call(
        near_dispatch, [(travel, BF), ((512, 256), BF)], 4, *table, own, near[1], near[2], near[4]
    )
    got_near = over_ctx(send_near)
    far = [swap(pair, "tp", 3), swap(near[4], "tp", 1), swap(near[4], "tp", 2)]
    send_far = call(far_dispatch, [(travel, BF)], 4, *table, *far, after=(send_near,))
    got_far = over_ctx(send_far)

    sums = ((slots, hidden_width), F32)
    dy_shape = ((QUAD, slots, 256), BF)
    act = ((slots, hidden_width), BF)
    gate, up, d_hidden, dy_near = call(
        near_kernel, [sums, sums, sums, dy_shape], 5, scalars, got_near,
        weights=(wg, wu, wd), wants=(NEAR,) * 3, after=(send_far,),
    )
    longer = (16, QUAD * 20 + 16, 256)
    hidden, d_gate, d_up, back_far, partial = call(
        far_kernel,
        [act, act, act, (longer, BF), ((hidden_width, width), BF)],
        8, scalars, got_far, gate, up, d_hidden, dy_near,
        weights=(wg, wu, wd), wants=(FAR + (4,),) * 3,
        more=(pltpu.VMEM((hidden_width, width), BF), pltpu.SemaphoreType.DMA((2 * QUAD,))),
        loose=1,
    )
    home_far = over_ctx(back_far)

    quarter = lax.psum_scatter(
        partial, "dp", scatter_dimension=0, axis_index_groups=[[0, 2, 4, 6], [1, 3, 5, 7]], tiled=True
    )
    back_near = call(
        back_kernel, [(travel, BF)], 4, scalars, hidden, d_gate, d_up,
        weights=(wg, wu, wd), wants=(LAST,) * 3,
    )
    home_near = over_ctx(back_near)

    part, longer = ((256, 256), BF), ((272, 256), BF)
    sums_far = call(
        functools.partial(combine_kernel, True), [longer] * 4, 4, *table, home_far,
        after=(back_near,),
    )
    came_far = [swap(sums_far[d], "tp", d) for d in (1, 2, 3)]
    end = ((96, width), BF)
    over = call(end_kernel, [end], 1, scalars, quarter, after=(sums_far[0],))
    ends = swap(over, "dp", 1)
    total_far = call(total_kernel, [longer], 1, scalars, sums_far[0], *came_far, after=(over,))
    from_far = swap(total_far, "tp", 4)
    sums_near = call(
        functools.partial(combine_kernel, False), [part] * 4, 4, *table, home_near,
        after=(total_far,),
    )
    came_near = [swap(sums_near[d], "tp", d) for d in (1, 2, 3)]
    flat = ((128, 256), BF)
    combined, grad_tokens, lines, grad_down = call(
        last_kernel, [flat, flat, (ids_t.shape, F32), end], 2,
        scalars, total_far, from_far, quarter, ends, sums_near[0], *came_near,
    )
    return combined, grad_tokens, lines.T, grad_down[None]


def solution(mesh):
    in_specs = (
        P(("dp", "ctx"), "tp"),
        P(("dp", "ctx"), "tp"),
        P(("dp", "ctx"), None),
        P(("dp", "ctx"), None),
        P(("ctx", "tp"), None, None),
        P(("ctx", "tp"), None, None),
        P(("ctx", "tp"), None, None),
    )
    out_specs = (
        P(("dp", "ctx"), "tp"),
        P(("dp", "ctx"), "tp"),
        P(("dp", "ctx"), None),
        P(("ctx", "tp"), "dp", None),
    )
    return jax.shard_map(shards, mesh=mesh, in_specs=in_specs, out_specs=out_specs, check_vma=False)
```
